32 devices in a mesh: group: 2 (over y), tensor: 4 (over z), dp: 4 (over x, core).
Axes of the slice: x: 2, y: 2, z: 4, core: 2. Of those that a mesh axis runs over, the one named last changes fastest.
Arguments:
- tokens: float32 [1920, 4096], P(('group', 'dp'), 'tensor'), parts along dimension 0, may hold values from -6 to 6
- cotangent: float32 [1920, 4096], P(('group', 'dp'), 'tensor'), parts along dimension 0, may hold values from -6 to 6
- w_up: float32 [288, 256, 256], P('tensor', 'dp'), may hold values from -0.1875 to 0.1875
- w_down: float32 [288, 256, 256], P('tensor', 'dp'), may hold values from -0.09375 to 0.09375
- block_col: int32 [4, 72], P('tensor'), may hold values from 0 to 15, as said below
- block_row: int32 [4, 72], P('tensor'), may hold values from 0 to 15
- block_count: int32 [4], P('tensor'), may hold values from 56 to 72, as said below
Outputs:
- mixed: float32 [1920, 4096], P(('group', 'dp'), 'tensor'), parts along dimension 0
- grad_tokens: float32 [1920, 4096], P(('group', 'dp'), 'tensor'), parts along dimension 0
- grad_up: float32 [576, 256, 256], P(('group', 'tensor'), 'dp'), parts along dimension 0
- grad_down: float32 [576, 256, 256], P(('group', 'tensor'), 'dp'), parts along dimension 0
The draws below stay inside these ranges and needn't reach their ends.
There are 2 independent parts, one for each index of `group`. The reference program is written for one: setup_inputs(seed, part) draws one part's arguments, and reference() takes and returns one part's arrays. A program takes and returns all parts, laid end to end along the dimension named above; an argument that names none is the same for every part. Nothing has to cross between parts.
Inputs may be any that keep to these rules, and one draw needn't show every extreme that they name: `block_col`: hidden block of each slot; within one index of tensor the first live slots name distinct pairs of hidden and model block. `block_count`: some index of tensor has all 72 slots live in every draw; the others have fewer or as many.
All inputs are finite; a program needn't handle non-finite values.
Results may differ from the reference program's by a relative error of at most 0.00013.
Values sent between devices are 32-bit elements; how exact they have to be, the bound alone decides.
A program may use at most 320 MiB of HBM per device.

```python
import jax
import jax.numpy as jnp
from jax import lax

D = 4096
FF = 16384
BLK = 256
HBLK = 16
DBLK = 16
CAP = 72
SLOTS = 288
TOKENS = 960
N_TENSOR = 4


def pair_table(key):
    keys = jax.random.split(key, N_TENSOR)

    def one_shard(shard_key):
        return jax.random.permutation(shard_key, HBLK * DBLK)[:CAP]
    return jax.vmap(one_shard)(keys).astype(jnp.int32)


def draw_block_col(key, part):
    return (pair_table(key) // DBLK).astype(jnp.int32)


def draw_block_row(key, part):
    return (pair_table(key) % DBLK).astype(jnp.int32)


def draw_block_count(key, part):
    key = jax.random.fold_in(key, 7)
    first_key, second_key = jax.random.split(key)
    counts = jax.random.randint(first_key, (N_TENSOR,), HBLK * 7 // 2, CAP + 1)
    fullest = jax.random.randint(second_key, (), 0, N_TENSOR)
    return jnp.where(jnp.arange(N_TENSOR) == fullest, CAP, counts).astype(jnp.int32)


def block_levels(stream_key, shape, pieces, smallest, top_value):
    loudness, own = 1.0, jax.random.fold_in(stream_key, 6)
    for dim, blocks in pieces:
        draws = jnp.exp(jax.random.uniform(jax.random.fold_in(own, dim), (blocks,), jnp.float32, smallest / len(pieces), top_value / len(pieces)))
        loudness = loudness * jnp.repeat(draws, shape[dim] // blocks).reshape([-1 if axis == dim else 1 for axis in range(len(shape))])
    return loudness


def bell_draw(own_key, shape, width, reach, cuts=(), kind=jnp.bfloat16):
    values = jax.random.normal(own_key, shape, jnp.float32) * width
    if len(cuts) > 0:
        values = block_levels(own_key, shape, cuts, -0.22, 0.18) * values
    return jnp.clip(values, min=-reach, max=reach).astype(kind)


def setup_inputs(seed: int = 0, part: int = 0) -> dict:
    splits = jax.random.split(jax.random.key(seed), 8)
    part_splits = jax.random.split(jax.random.fold_in(splits[7], part), 8)
    return {
        "tokens": bell_draw(part_splits[0], (TOKENS, D), 1.0, 6.0, ((0, 4), (1, 4)), jnp.float32),
        "cotangent": bell_draw(part_splits[1], (TOKENS, D), 1.0, 6.0, ((0, 4), (1, 4)), jnp.float32),
        "w_up": bell_draw(splits[2], (SLOTS, BLK, BLK), (4 * BLK) ** -0.5, 0.1875, ((0, 4), (1, 4)), jnp.float32),
        "w_down": bell_draw(splits[3], (SLOTS, BLK, BLK), (FF // 4) ** -0.5, 0.09375, ((0, 4), (1, 4)), jnp.float32),
        "block_col": draw_block_col(jax.random.fold_in(splits[7], 71), part),
        "block_row": draw_block_row(jax.random.fold_in(splits[7], 71), part),
        "block_count": draw_block_count(jax.random.fold_in(splits[7], 71), part),
    }


precise = lax.Precision.HIGHEST

def gelu_tanh(values):
    return jax.nn.gelu(values, approximate=True)

def slot_tables(block_col, block_row, block_count):
    shards = block_col.shape[0]
    slot_num = block_col.shape[1]
    alive_slots = (jnp.arange(slot_num, dtype=jnp.int32)[None, :] < block_count[:, None]).astype(jnp.float32)
    global_col = block_col + jnp.arange(shards, dtype=jnp.int32)[:, None] * HBLK
    alive_flat = alive_slots.reshape(-1)
    col_onehot = (global_col.reshape(-1)[:, None] == jnp.arange(HBLK * shards, dtype=jnp.int32)[None, :]).astype(jnp.float32) * alive_flat[:, None]
    row_onehot = (block_row.reshape(-1)[:, None] == jnp.arange(DBLK, dtype=jnp.int32)[None, :]).astype(jnp.float32) * alive_flat[:, None]
    return (col_onehot, row_onehot)

def reference(tokens, cotangent, w_up, w_down, block_col, block_row, block_count):
    col_onehot, row_onehot = slot_tables(block_col, block_row, block_count)
    rows_all = tokens.shape[0]

    def forward(token_data, up_tiles, down_tiles):
        picked = jnp.einsum('trb,sr->tsb', token_data.reshape(rows_all, DBLK, BLK), row_onehot, precision=precise)
        upper = jnp.einsum('tsb,sbe->tse', picked, up_tiles, precision=precise)
        hidden = jnp.einsum('tse,sf->tfe', upper, col_onehot, precision=precise)
        activ = gelu_tanh(hidden)
        act_pick = jnp.einsum('tfe,sf->tse', activ, col_onehot, precision=precise)
        down_terms = jnp.einsum('tse,sed->tsd', act_pick, down_tiles, precision=precise)
        return jnp.einsum('tsd,sr->trd', down_terms, row_onehot, precision=precise).reshape(rows_all, DBLK * BLK)
    mixed, pullback = jax.vjp(forward, tokens, w_up, w_down)
    grad_tokens, grad_up, grad_down = pullback(cotangent)
    return (mixed, grad_tokens, grad_up, grad_down)
```

```python
import functools

import jax
import jax.numpy as jnp
from jax import lax
from jax.experimental import pallas as pl
from jax.experimental.pallas import tpu as pltpu
from jax.sharding import PartitionSpec as P

FF = 16384
CUBIC = 0.044715
SCALE = 0.7978845608028654
F32 = jnp.float32
BF16 = jnp.bfloat16


def split(v):
    high = v.astype(BF16)
    return high, (v - high.astype(F32)).astype(BF16)


def mm(a, b, ca, cb):
    dims = (((ca,), (cb,)), ((), ()))
    dot = functools.partial(lax.dot_general, dimension_numbers=dims, preferred_element_type=F32)
    return dot(a[0], b[0]) + (dot(a[0], b[1]) + dot(a[1], b[0]))


def feature(ref, block, per, size):
    if per == 1:
        return ref.at[block]
    at = pl.multiple_of((block % per) * size, size)
    return ref.at[block // per, :, pl.ds(at, size)]


def fill(refs, inits):
    for ref, init in zip(refs, inits):
        def one(i, carry, ref=ref, init=init):
            ref[i] = jnp.zeros(ref.shape[1:], ref.dtype) if init is None else init[i]
            return carry

        lax.fori_loop(0, ref.shape[0], one, 0)


def load_tile(pieces, offs, j, high, low):
    for p, piece in enumerate(pieces):
        rows = piece.shape[1]
        h, l = split(piece[j])
        at = pl.ds(pl.multiple_of(offs[p], rows), rows)
        high[j, at, :] = h
        low[j, at, :] = l
    return high[j], low[j]


def up_kernel(cfg, table, offs, tok, *refs):
    base, n, per, size, pieces_n, first, final = cfg
    pieces, refs = refs[:pieces_n], refs[pieces_n:]
    init = None
    if not first:
        init, refs = refs[0], refs[1:]
    if final:
        act, slope, high, low, acc = refs
    else:
        acc, high, low = refs
    step = pl.program_id(0)

    @pl.when(step == 0)
    def _():
        fill([acc], [init])

    for j in range(n):
        s = base + step * n + j
        q, r = table[0, s], table[1, s]
        live = jnp.where(s < table[2, 0], 1.0, 0.0).astype(F32)
        tile = load_tile(pieces, offs, j, high, low)
        acc[q] += live * mm(split(feature(tok, r, per, size)[...]), tile, 1, 0)

    if final:
        @pl.when(step == pl.num_programs(0) - 1)
        def _():
            def one(i, carry):
                v = acc[i]
                t = jnp.tanh(SCALE * (v + CUBIC * (v * v * v)))
                act[i] = 0.5 * v * (1.0 + t)
                slope[i] = 0.5 * (1.0 + t) + (0.5 * SCALE) * v * (1.0 - t * t) * (
                    1.0 + (3.0 * CUBIC) * (v * v)
                )
                return carry

            lax.fori_loop(0, acc.shape[0], one, 0)


def emit_grad(out_pieces, offs, start, j, g_scr, g):
    g_scr[j] = g
    for p, out in enumerate(out_pieces):
        rows = out.shape[1]
        out[j] = g_scr[j, pl.ds(pl.multiple_of(offs[start + p], rows), rows), :]


def down_kernel(cfg, out_n, table, offs, act, slope, cot, *refs):
    base, n, per, size, pieces_n, first, final = cfg
    pieces, refs = refs[:pieces_n], refs[pieces_n:]
    inits = (None, None)
    if not first:
        inits, refs = refs[:2], refs[2:]
    mixed, back = refs[:2]
    outs, (high, low, g_scr) = refs[2:2 + out_n], refs[2 + out_n:]
    step = pl.program_id(0)

    @pl.when(step == 0)
    def _():
        fill([mixed, back], inits)

    for j in range(n):
        s = base + step * n + j
        q, r = table[0, s], table[1, s]
        live = jnp.where(s < table[2, 0], 1.0, 0.0).astype(F32)
        tile = load_tile(pieces, offs, j, high, low)
        a = split(act[q])
        b = split(feature(cot, r, per, size)[...])
        emit_grad(outs, offs, pieces_n, j, g_scr, live * mm(a, b, 0, 0))
        back[q] += live * mm(b, tile, 1, 1)
        place = feature(mixed, r, per, size)
        place[...] += live * mm(a, tile, 1, 0)

    if final:
        @pl.when(step == pl.num_programs(0) - 1)
        def _():
            def one(i, carry):
                back[i] = back[i] * slope[i]
                return carry

            lax.fori_loop(0, back.shape[0], one, 0)


def end_kernel(cfg, out_n, table, offs, tok, gh, *refs):
    base, n, per, size, pieces_n, first, final = cfg
    pieces, refs = refs[:pieces_n], refs[pieces_n:]
    init = None
    if not first:
        init, refs = refs[0], refs[1:]
    grad = refs[0]
    outs, (high, low, g_scr) = refs[1:1 + out_n], refs[1 + out_n:]
    step = pl.program_id(0)

    @pl.when(step == 0)
    def _():
        fill([grad], [init])

    for j in range(n):
        s = base + step * n + j
        q, r = table[0, s], table[1, s]
        live = jnp.where(s < table[2, 0], 1.0, 0.0).astype(F32)
        tile = load_tile(pieces, offs, j, high, low)
        a = split(feature(tok, r, per, size)[...])
        b = split(gh[q])
        emit_grad(outs, offs, pieces_n, j, g_scr, live * mm(a, b, 0, 0))
        place = feature(grad, r, per, size)
        place[...] += live * mm(b, tile, 1, 1)


def call(kernel, table, offs, whole_in, pieces, inits, whole_out, out_rows, n, size, scratch, flops):
    slots = pieces[0].shape[0]

    def whole(shape):
        return pl.BlockSpec(shape, lambda i, *_: (0,) * len(shape), pipeline_mode=pl.Buffered(1))

    def part(rows):
        return pl.BlockSpec((n, rows, size), lambda i, *_: (i, 0, 0))

    args = list(whole_in) + list(pieces) + list(inits)
    moved = sum(a.size for a in args) * 4 + 4 * sum(
        slots * rows * size for rows in out_rows
    ) + 4 * sum(functools.reduce(lambda x, y: x * y, s) for s in whole_out)
    return pl.pallas_call(
        kernel,
        grid_spec=pltpu.PrefetchScalarGridSpec(
            num_scalar_prefetch=2,
            grid=(slots // n,),
            in_specs=[whole(a.shape) for a in whole_in]
            + [part(p.shape[1]) for p in pieces]
            + [whole(a.shape) for a in inits],
            out_specs=[whole(s) for s in whole_out] + [part(rows) for rows in out_rows],
            scratch_shapes=scratch,
        ),
        out_shape=[jax.ShapeDtypeStruct(s, F32) for s in whole_out]
        + [jax.ShapeDtypeStruct((slots, rows, size), F32) for rows in out_rows],
        compiler_params=pltpu.CompilerParams(
            dimension_semantics=("arbitrary",), vmem_limit_bytes=56 * 1024 * 1024
        ),
        cost_estimate=pl.CostEstimate(flops=flops, bytes_accessed=moved, transcendentals=0),
    )(table, offs, *args)


def on_device(groups, dps, tokens, cotangent, w_up, w_down, block_col, block_row, block_count):
    slots, rows_w, size = w_up.shape
    rows, width = tokens.shape
    tensor = lax.axis_size("tensor")
    per = width // size
    hidden = FF // (size * tensor)
    paired = groups == 2 and dps == 4 and slots % 8 == 0
    chunks = 2 if paired else 1
    count = slots // chunks
    n = max(k for k in (1, 2, 3, 4) if count % k == 0)

    table = jnp.stack([block_col[0], block_row[0], jnp.broadcast_to(block_count, (slots,))])
    d = lax.axis_index("dp")
    if paired:
        y = lax.axis_index("group")
        half = rows_w // 2
        other_core, other_x = d + 1 - 2 * (d % 2), (d + 2) % 4
        other_both = other_core + 2 - 4 * (other_core // 2)

        def over_core(v):
            return lax.ppermute(v, "dp", [(0, 1), (1, 0), (2, 3), (3, 2)])

        def over_x(v):
            return lax.ppermute(v, "dp", [(0, 2), (2, 0), (1, 3), (3, 1)])

        def over_y(v):
            return lax.ppermute(v, "group", [(0, 1), (1, 0)])

        def gather(w):
            near = lax.dynamic_slice_in_dim(w, y * half, half, axis=1)
            by_x = over_x(near)
            by_y = over_y(by_x)
            return (w, over_core(w), by_x, by_y, over_core(by_x), over_core(by_y))

        offs = jnp.stack(
            [
                d * rows_w,
                other_core * rows_w,
                other_x * rows_w + y * half,
                other_x * rows_w + (1 - y) * half,
                other_both * rows_w + y * half,
                other_both * rows_w + (1 - y) * half,
                d * rows_w,
                other_x * rows_w,
                other_core * rows_w,
                other_both * rows_w,
            ]
        ).astype(jnp.int32)
        out_rows = (rows_w,) * 4

        def scatter(mine, to_x, to_core, to_both):
            far = over_x(to_x + over_core(to_both))
            return mine + over_core(to_core), far
    else:
        offs = jnp.zeros((2,), jnp.int32)
        out_rows = (size,)

        def gather(w):
            return (lax.all_gather(w, "dp", axis=1, tiled=True),)

        def scatter(whole):
            return (lax.psum_scatter(whole, "dp", scatter_dimension=1, tiled=True),)

    full_tokens = lax.all_gather(tokens, "tensor")
    ups = [gather(w_up[c * count:(c + 1) * count]) for c in range(chunks)]
    downs = [gather(w_down[c * count:(c + 1) * count]) for c in range(chunks)]
    full_cot = lax.all_gather(cotangent, "tensor")

    acts = (hidden, rows, size)
    feats = (tensor, rows, width)
    tiles = [pltpu.VMEM((n, size, size), BF16), pltpu.VMEM((n, size, size), BF16)]
    g_tile = [pltpu.VMEM((n, size, size), F32)]
    product = 6 * count * rows * size * size

    def cfg(c):
        return (c * count, n, per, size, len(ups[c]), c == 0, c == chunks - 1)

    state = []
    for c in range(chunks):
        last = c == chunks - 1
        state = call(
            functools.partial(up_kernel, cfg(c)), table, offs, [full_tokens], ups[c], state,
            [acts, acts] if last else [acts], (), n, size,
            tiles + ([pltpu.VMEM(acts, F32)] if last else []), product,
        )
    act, slope = state

    state, down_grads = [], []
    for c in range(chunks):
        mixed, back, *parts = call(
            functools.partial(down_kernel, cfg(c), len(out_rows)), table, offs,
            [act, slope, full_cot], downs[c], state, [feats, acts], out_rows, n, size,
            tiles + g_tile, 3 * product,
        )
        state = [mixed, back]
        down_grads.append(scatter(*parts))
    mixed_out = lax.psum_scatter(mixed, "tensor", scatter_dimension=0)

    state, up_grads = [], []
    for c in range(chunks):
        grad, *parts = call(
            functools.partial(end_kernel, cfg(c), len(out_rows)), table, offs,
            [full_tokens, back], ups[c], state, [feats], out_rows, n, size,
            tiles + g_tile, 2 * product,
        )
        state = [grad]
        up_grads.append(scatter(*parts))
    grad_tokens = lax.psum_scatter(grad, "tensor", scatter_dimension=0)

    def join(grads):
        return jnp.concatenate([sum(g[1:], g[0]) for g in grads], axis=0)

    return mixed_out, grad_tokens, join(up_grads), join(down_grads)


def solution(mesh):
    in_specs = (
        P(("group", "dp"), "tensor"),
        P(("group", "dp"), "tensor"),
        P("tensor", "dp", None),
        P("tensor", "dp", None),
        P("tensor", None),
        P("tensor", None),
        P("tensor"),
    )
    out_specs = (
        P(("group", "dp"), "tensor"),
        P(("group", "dp"), "tensor"),
        P(("group", "tensor"), "dp", None),
        P(("group", "tensor"), "dp", None),
    )
    return jax.shard_map(
        functools.partial(on_device, mesh.shape["group"], mesh.shape["dp"]),
        mesh=mesh, in_specs=in_specs, out_specs=out_specs, check_vma=False,
    )
```

```python
import functools

import jax
import jax.numpy as jnp
from jax import lax
from jax.experimental import pallas as pl
from jax.experimental.pallas import tpu as pltpu
from jax.sharding import PartitionSpec as P

FF = 16384
CUBIC = 0.044715
SCALE = 0.7978845608028654
F32 = jnp.float32
BF16 = jnp.bfloat16


def split(v):
    high = v.astype(BF16)
    return high, (v - high.astype(F32)).astype(BF16)


def mm(a, b, ca, cb):
    dims = (((ca,), (cb,)), ((), ()))
    dot = functools.partial(lax.dot_general, dimension_numbers=dims, preferred_element_type=F32)
    return dot(a[0], b[0]) + (dot(a[0], b[1]) + dot(a[1], b[0]))


def feature(ref, block, per, size):
    if per == 1:
        return ref.at[block]
    at = pl.multiple_of((block % per) * size, size)
    return ref.at[block // per, :, pl.ds(at, size)]


def fill(refs, inits):
    for ref, init in zip(refs, inits):
        def one(i, carry, ref=ref, init=init):
            ref[i] = jnp.zeros(ref.shape[1:], ref.dtype) if init is None else init[i]
            return carry

        lax.fori_loop(0, ref.shape[0], one, 0)


def load_tile(pieces, offs, j, high, low):
    for p, piece in enumerate(pieces):
        rows = piece.shape[1]
        h, l = split(piece[j])
        at = pl.ds(pl.multiple_of(offs[p], rows), rows)
        high[j, at, :] = h
        low[j, at, :] = l
    return high[j], low[j]


def up_kernel(cfg, table, offs, tok, *refs):
    base, n, per, size, pieces_n, first, final = cfg
    pieces, refs = refs[:pieces_n], refs[pieces_n:]
    init = None
    if not first:
        init, refs = refs[0], refs[1:]
    if final:
        act, slope, high, low, acc = refs
    else:
        acc, high, low = refs
    step = pl.program_id(0)

    @pl.when(step == 0)
    def _():
        fill([acc], [init])

    for j in range(n):
        s = base + step * n + j
        q, r = table[0, s], table[1, s]
        live = jnp.where(s < table[2, 0], 1.0, 0.0).astype(F32)
        tile = load_tile(pieces, offs, j, high, low)
        acc[q] += live * mm(split(feature(tok, r, per, size)[...]), tile, 1, 0)

    if final:
        @pl.when(step == pl.num_programs(0) - 1)
        def _():
            def one(i, carry):
                v = acc[i]
                t = jnp.tanh(SCALE * (v + CUBIC * (v * v * v)))
                act[i] = 0.5 * v * (1.0 + t)
                slope[i] = 0.5 * (1.0 + t) + (0.5 * SCALE) * v * (1.0 - t * t) * (
                    1.0 + (3.0 * CUBIC) * (v * v)
                )
                return carry

            lax.fori_loop(0, acc.shape[0], one, 0)


def emit_grad(out_pieces, offs, start, j, g_scr, g):
    g_scr[j] = g
    for p, out in enumerate(out_pieces):
        rows = out.shape[1]
        out[j] = g_scr[j, pl.ds(pl.multiple_of(offs[start + p], rows), rows), :]


def down_kernel(cfg, out_n, table, offs, act, slope, cot, *refs):
    base, n, per, size, pieces_n, first, final = cfg
    pieces, refs = refs[:pieces_n], refs[pieces_n:]
    inits = (None, None)
    if not first:
        inits, refs = refs[:2], refs[2:]
    mixed, back = refs[:2]
    outs, (high, low, g_scr) = refs[2:2 + out_n], refs[2 + out_n:]
    step = pl.program_id(0)

    @pl.when(step == 0)
    def _():
        fill([mixed, back], inits)

    for j in range(n):
        s = base + step * n + j
        q, r = table[0, s], table[1, s]
        live = jnp.where(s < table[2, 0], 1.0, 0.0).astype(F32)
        tile = load_tile(pieces, offs, j, high, low)
        a = split(act[q])
        b = split(feature(cot, r, per, size)[...])
        emit_grad(outs, offs, pieces_n, j, g_scr, live * mm(a, b, 0, 0))
        back[q] += live * mm(b, tile, 1, 1)
        place = feature(mixed, r, per, size)
        place[...] += live * mm(a, tile, 1, 0)

    if final:
        @pl.when(step == pl.num_programs(0) - 1)
        def _():
            def one(i, carry):
                back[i] = back[i] * slope[i]
                return carry

            lax.fori_loop(0, back.shape[0], one, 0)


def end_kernel(cfg, out_n, table, offs, tok, gh, *refs):
    base, n, per, size, pieces_n, first, final = cfg
    pieces, refs = refs[:pieces_n], refs[pieces_n:]
    init = None
    if not first:
        init, refs = refs[0], refs[1:]
    grad = refs[0]
    outs, (high, low, g_scr) = refs[1:1 + out_n], refs[1 + out_n:]
    step = pl.program_id(0)

    @pl.when(step == 0)
    def _():
        fill([grad], [init])

    for j in range(n):
        s = base + step * n + j
        q, r = table[0, s], table[1, s]
        live = jnp.where(s < table[2, 0], 1.0, 0.0).astype(F32)
        tile = load_tile(pieces, offs, j, high, low)
        a = split(feature(tok, r, per, size)[...])
        b = split(gh[q])
        emit_grad(outs, offs, pieces_n, j, g_scr, live * mm(a, b, 0, 0))
        place = feature(grad, r, per, size)
        place[...] += live * mm(b, tile, 1, 1)


def call(kernel, table, offs, whole_in, pieces, inits, whole_out, out_rows, n, size, scratch, flops,
         lo, slots):
    skip = lo // n

    def whole(shape):
        return pl.BlockSpec(shape, lambda i, *_: (0,) * len(shape), pipeline_mode=pl.Buffered(1))

    def part(rows, ahead=0):
        return pl.BlockSpec((n, rows, size), lambda i, *_: (i + ahead, 0, 0))

    args = list(whole_in) + list(pieces) + list(inits)
    moved = sum(a.size for a in list(whole_in) + list(inits)) * 4 + 4 * slots * size * size + 4 * sum(
        slots * rows * size for rows in out_rows
    ) + 4 * sum(functools.reduce(lambda x, y: x * y, s) for s in whole_out)
    return pl.pallas_call(
        kernel,
        grid_spec=pltpu.PrefetchScalarGridSpec(
            num_scalar_prefetch=2,
            grid=(slots // n,),
            in_specs=[whole(a.shape) for a in whole_in]
            + [part(p.shape[1], skip) for p in pieces]
            + [whole(a.shape) for a in inits],
            out_specs=[whole(s) for s in whole_out] + [part(rows) for rows in out_rows],
            scratch_shapes=scratch,
        ),
        out_shape=[jax.ShapeDtypeStruct(s, F32) for s in whole_out]
        + [jax.ShapeDtypeStruct((slots, rows, size), F32) for rows in out_rows],
        compiler_params=pltpu.CompilerParams(
            dimension_semantics=("arbitrary",), vmem_limit_bytes=56 * 1024 * 1024
        ),
        cost_estimate=pl.CostEstimate(flops=flops, bytes_accessed=moved, transcendentals=0),
    )(table, offs, *args)


def on_device(groups, dps, tokens, cotangent, w_up, w_down, block_col, block_row, block_count):
    slots, rows_w, size = w_up.shape
    rows, width = tokens.shape
    tensor = lax.axis_size("tensor")
    per = width // size
    hidden = FF // (size * tensor)
    paired = groups == 2 and dps == 4 and slots % 24 == 0
    chunks = 2 if paired else 1
    count = slots // chunks
    n = max(k for k in (1, 2, 3, 4) if (count // 3 if paired else count) % k == 0)

    def after(value, *others):
        return lax.optimization_barrier((value, *others))[0]

    table = jnp.stack([block_col[0], block_row[0], jnp.broadcast_to(block_count, (slots,))])
    d = lax.axis_index("dp")
    if paired:
        y = lax.axis_index("group")
        half = rows_w // 2
        other_core, other_x = d + 1 - 2 * (d % 2), (d + 2) % 4
        other_both = other_core + 2 - 4 * (other_core // 2)

        def over_core(v):
            return lax.ppermute(v, "dp", [(0, 1), (1, 0), (2, 3), (3, 2)])

        def over_x(v):
            return lax.ppermute(v, "dp", [(0, 2), (2, 0), (1, 3), (3, 1)])

        def over_y(v):
            return lax.ppermute(v, "group", [(0, 1), (1, 0)])

        def gather(w, *ahead):
            near = lax.dynamic_slice_in_dim(w, y * half, half, axis=1)
            return (w, over_core(w), over_x(after(near, *ahead)))

        def spread(w, by_core, by_x):
            by_y = over_y(by_x)
            return (w, by_core, by_x, by_y, over_core(by_x), by_y)

        offs = jnp.stack(
            [
                d * rows_w,
                other_core * rows_w,
                other_x * rows_w + y * half,
                other_x * rows_w + (1 - y) * half,
                other_both * rows_w + y * half,
                other_both * rows_w + (1 - y) * half,
                d * rows_w,
                other_x * rows_w,
                other_core * rows_w,
            ]
            + [other_both * rows_w + k * (rows_w // 4) for k in range(4)]
        ).astype(jnp.int32)
        out_rows = (rows_w,) * 3 + (rows_w // 4,) * 4

        def scatter(mine, to_x, to_core, *to_both):
            summed = to_x + jnp.concatenate([over_core(v) for v in to_both], axis=1)
            return summed, (over_x(summed), mine, over_core(to_core))
    else:
        offs = jnp.zeros((2,), jnp.int32)
        out_rows = (size,)

        def gather(w, *ahead):
            return (lax.all_gather(w, "dp", axis=1, tiled=True),)

        def spread(whole):
            return (whole,)

        def scatter(whole):
            return whole, (lax.psum_scatter(whole, "dp", scatter_dimension=1, tiled=True),)

    full_tokens = lax.all_gather(tokens, "tensor")
    ups = [gather(w_up[c * count:(c + 1) * count]) for c in range(chunks)]
    downs = [gather(w_down[c * count:(c + 1) * count], ups[c][-1]) for c in range(chunks)]
    full_cot = lax.all_gather(cotangent, "tensor")

    acts = (hidden, rows, size)
    feats = (tensor, rows, width)
    tiles = [pltpu.VMEM((n, size, size), BF16), pltpu.VMEM((n, size, size), BF16)]
    g_tile = [pltpu.VMEM((n, size, size), F32)]
    product = 6 * rows * size * size

    def cfg(c, lo, first, last):
        return (c * count + lo, n, per, size, len(ups[0]), first, last)

    ups, downs = [spread(*u) for u in ups], [spread(*u) for u in downs]
    if paired:
        ups = [(*u[:-1], over_core(u[-1])) for u in ups]
    state = []
    for c in range(chunks):
        last = c == chunks - 1
        state = call(
            functools.partial(up_kernel, cfg(c, 0, c == 0, last)),
            after(table, downs[c][2]) if paired else table, offs, [full_tokens],
            ups[c], state, [acts, acts] if last else [acts], (), n, size,
            tiles + ([pltpu.VMEM(acts, F32)] if last else []), count * product, 0, count,
        )
    act, slope = state
    if paired:
        downs = [(*u[:-1], over_core(after(u[-1], act))) for u in downs]

    sums, sent = [], []

    def gate():
        waits = sums[-1:] + [g[0] for g in sent[-2:-1]]
        return after(table, *(waits or downs[-1][1:])) if paired else table

    third = count // 3
    whole = [(c, 0, count) for c in range(chunks)]
    cuts = [(0, 0, third), (0, third, count - third)] + whole[1:] if paired else whole
    state = []
    for c, lo, num in cuts:
        last = c == chunks - 1
        mixed, back, *parts = call(
            functools.partial(down_kernel, cfg(c, lo, not state, last), len(out_rows)),
            gate(), offs, [act, slope, full_cot], downs[c], state, [feats, acts], out_rows, n, size,
            tiles + g_tile, 3 * num * product, lo, num,
        )
        state = [mixed, back]
        summed, grads = scatter(*parts)
        sums.append(summed)
        sent.append(grads)
    mixed_out = lax.psum_scatter(mixed, "tensor", scatter_dimension=0)

    state = []
    for c, lo, num in cuts:
        grad, *parts = call(
            functools.partial(end_kernel, cfg(c, lo, not state, False), len(out_rows)),
            gate(), offs, [full_tokens, back], ups[c], state, [feats], out_rows, n, size,
            tiles + g_tile, 2 * num * product, lo, num,
        )
        state = [grad]
        summed, grads = scatter(*parts)
        sums.append(summed)
        sent.append(grads)
    grad_tokens = lax.psum_scatter(grad, "tensor", scatter_dimension=0)

    def join(grads):
        return jnp.concatenate([sum(g[1:], g[0]) for g in grads], axis=0)

    return mixed_out, grad_tokens, join(sent[len(cuts):]), join(sent[:len(cuts)])


def solution(mesh):
    in_specs = (
        P(("group", "dp"), "tensor"),
        P(("group", "dp"), "tensor"),
        P("tensor", "dp", None),
        P("tensor", "dp", None),
        P("tensor", None),
        P("tensor", None),
        P("tensor"),
    )
    out_specs = (
        P(("group", "dp"), "tensor"),
        P(("group", "dp"), "tensor"),
        P(("group", "tensor"), "dp", None),
        P(("group", "tensor"), "dp", None),
    )
    return jax.shard_map(
        functools.partial(on_device, mesh.shape["group"], mesh.shape["dp"]),
        mesh=mesh, in_specs=in_specs, out_specs=out_specs, check_vma=False,
    )
```

```python
import functools

import jax
import jax.numpy as jnp
from jax import lax
from jax.experimental import pallas as pl
from jax.experimental.pallas import tpu as pltpu
from jax.sharding import PartitionSpec as P

FF = 16384
CUBIC = 0.044715
SCALE = 0.7978845608028654
F32 = jnp.float32
BF16 = jnp.bfloat16


def split(v):
    high = v.astype(BF16)
    return high, (v - high.astype(F32)).astype(BF16)


def mm(a, b, ca, cb):
    dims = (((ca,), (cb,)), ((), ()))
    dot = functools.partial(lax.dot_general, dimension_numbers=dims, preferred_element_type=F32)
    return dot(a[0], b[0]) + (dot(a[0], b[1]) + dot(a[1], b[0]))


def feature(ref, block, per, size):
    if per == 1:
        return ref.at[block]
    at = pl.multiple_of((block % per) * size, size)
    return ref.at[block // per, :, pl.ds(at, size)]


def fill(refs, inits):
    for ref, init in zip(refs, inits):
        def one(i, carry, ref=ref, init=init):
            ref[i] = jnp.zeros(ref.shape[1:], ref.dtype) if init is None else init[i]
            return carry

        lax.fori_loop(0, ref.shape[0], one, 0)


def load_tile(pieces, offs, j, high, low):
    for p, piece in enumerate(pieces):
        rows = piece.shape[1]
        h, l = split(piece[j])
        at = pl.ds(pl.multiple_of(offs[p], rows), rows)
        high[j, at, :] = h
        low[j, at, :] = l
    return high[j], low[j]


def up_kernel(cfg, table, offs, tok, *refs):
    base, n, per, size, pieces_n, first, final = cfg
    pieces, refs = refs[:pieces_n], refs[pieces_n:]
    init = None
    if not first:
        init, refs = refs[0], refs[1:]
    if final:
        act, slope, high, low, acc = refs
    else:
        acc, high, low = refs
    step = pl.program_id(0)

    @pl.when(step == 0)
    def _():
        fill([acc], [init])

    for j in range(n):
        s = base + step * n + j
        q, r = table[0, s], table[1, s]
        live = jnp.where(s < table[2, 0], 1.0, 0.0).astype(F32)
        tile = load_tile(pieces, offs, j, high, low)
        acc[q] += live * mm(split(feature(tok, r, per, size)[...]), tile, 1, 0)

    if final:
        @pl.when(step == pl.num_programs(0) - 1)
        def _():
            def one(i, carry):
                v = acc[i]
                t = jnp.tanh(SCALE * (v + CUBIC * (v * v * v)))
                act[i] = 0.5 * v * (1.0 + t)
                slope[i] = 0.5 * (1.0 + t) + (0.5 * SCALE) * v * (1.0 - t * t) * (
                    1.0 + (3.0 * CUBIC) * (v * v)
                )
                return carry

            lax.fori_loop(0, acc.shape[0], one, 0)


def emit_grad(out_pieces, offs, start, j, g_scr, g):
    g_scr[j] = g
    for p, out in enumerate(out_pieces):
        rows = out.shape[1]
        out[j] = g_scr[j, pl.ds(pl.multiple_of(offs[start + p], rows), rows), :]


def down_kernel(cfg, out_n, table, offs, act, slope, cot, *refs):
    base, n, per, size, pieces_n, first, final = cfg
    pieces, refs = refs[:pieces_n], refs[pieces_n:]
    inits = (None, None)
    if not first:
        inits, refs = refs[:2], refs[2:]
    mixed, back = refs[:2]
    outs, (high, low, g_scr) = refs[2:2 + out_n], refs[2 + out_n:]
    step = pl.program_id(0)

    @pl.when(step == 0)
    def _():
        fill([mixed, back], inits)

    for j in range(n):
        s = base + step * n + j
        q, r = table[0, s], table[1, s]
        live = jnp.where(s < table[2, 0], 1.0, 0.0).astype(F32)
        tile = load_tile(pieces, offs, j, high, low)
        a = split(act[q])
        b = split(feature(cot, r, per, size)[...])
        emit_grad(outs, offs, pieces_n, j, g_scr, live * mm(a, b, 0, 0))
        back[q] += live * mm(b, tile, 1, 1)
        place = feature(mixed, r, per, size)
        place[...] += live * mm(a, tile, 1, 0)

    if final:
        @pl.when(step == pl.num_programs(0) - 1)
        def _():
            def one(i, carry):
                back[i] = back[i] * slope[i]
                return carry

            lax.fori_loop(0, back.shape[0], one, 0)


def end_kernel(cfg, out_n, table, offs, tok, gh, *refs):
    base, n, per, size, pieces_n, first, final = cfg
    pieces, refs = refs[:pieces_n], refs[pieces_n:]
    init = None
    if not first:
        init, refs = refs[0], refs[1:]
    grad = refs[0]
    outs, (high, low, g_scr) = refs[1:1 + out_n], refs[1 + out_n:]
    step = pl.program_id(0)

    @pl.when(step == 0)
    def _():
        fill([grad], [init])

    for j in range(n):
        s = base + step * n + j
        q, r = table[0, s], table[1, s]
        live = jnp.where(s < table[2, 0], 1.0, 0.0).astype(F32)
        tile = load_tile(pieces, offs, j, high, low)
        a = split(feature(tok, r, per, size)[...])
        b = split(gh[q])
        emit_grad(outs, offs, pieces_n, j, g_scr, live * mm(a, b, 0, 0))
        place = feature(grad, r, per, size)
        place[...] += live * mm(b, tile, 1, 1)


def call(kernel, table, offs, whole_in, pieces, inits, whole_out, out_rows, n, size, scratch, flops,
         lo, slots):
    skip = lo // n

    def whole(shape):
        return pl.BlockSpec(shape, lambda i, *_: (0,) * len(shape), pipeline_mode=pl.Buffered(1))

    def part(rows, ahead=0):
        return pl.BlockSpec((n, rows, size), lambda i, *_: (i + ahead, 0, 0))

    args = list(whole_in) + list(pieces) + list(inits)
    moved = sum(a.size for a in list(whole_in) + list(inits)) * 4 + 4 * slots * size * size + 4 * sum(
        slots * rows * size for rows in out_rows
    ) + 4 * sum(functools.reduce(lambda x, y: x * y, s) for s in whole_out)
    return pl.pallas_call(
        kernel,
        grid_spec=pltpu.PrefetchScalarGridSpec(
            num_scalar_prefetch=2,
            grid=(slots // n,),
            in_specs=[whole(a.shape) for a in whole_in]
            + [part(p.shape[1], skip) for p in pieces]
            + [whole(a.shape) for a in inits],
            out_specs=[whole(s) for s in whole_out] + [part(rows) for rows in out_rows],
            scratch_shapes=scratch,
        ),
        out_shape=[jax.ShapeDtypeStruct(s, F32) for s in whole_out]
        + [jax.ShapeDtypeStruct((slots, rows, size), F32) for rows in out_rows],
        compiler_params=pltpu.CompilerParams(
            dimension_semantics=("arbitrary",), vmem_limit_bytes=56 * 1024 * 1024
        ),
        cost_estimate=pl.CostEstimate(flops=flops, bytes_accessed=moved, transcendentals=0),
    )(table, offs, *args)


def on_device(groups, dps, tokens, cotangent, w_up, w_down, block_col, block_row, block_count):
    slots, rows_w, size = w_up.shape
    rows, width = tokens.shape
    tensor = lax.axis_size("tensor")
    per = width // size
    hidden = FF // (size * tensor)
    paired = groups == 2 and dps == 4 and slots % 24 == 0
    chunks = 2 if paired else 1
    sums, sent = [], []
    count = slots // chunks
    n = max(k for k in (1, 2, 3, 4) if (count // 3 if paired else count) % k == 0)

    def after(value, *others):
        return lax.optimization_barrier((value, *others))[0]

    table = jnp.stack([block_col[0], block_row[0], jnp.broadcast_to(block_count, (slots,))])
    d = lax.axis_index("dp")
    if paired:
        y = lax.axis_index("group")
        half = rows_w // 2
        other_core, other_x = d + 1 - 2 * (d % 2), (d + 2) % 4
        other_both = other_core + 2 - 4 * (other_core // 2)

        def over_core(v):
            return lax.ppermute(v, "dp", [(0, 1), (1, 0), (2, 3), (3, 2)])

        def over_x(v):
            return lax.ppermute(v, "dp", [(0, 2), (2, 0), (1, 3), (3, 1)])

        def over_y(v):
            return lax.ppermute(v, "group", [(0, 1), (1, 0)])

        def gather(w, *ahead):
            near = lax.dynamic_slice_in_dim(w, y * half, half, axis=1)
            return (w, over_core(w), over_x(after(near, *ahead)))

        def spread(w, by_core, by_x):
            by_y = over_y(by_x)
            return (w, by_core, by_x, by_y, over_core(by_x), by_y)

        offs = jnp.stack(
            [
                d * rows_w,
                other_core * rows_w,
                other_x * rows_w + y * half,
                other_x * rows_w + (1 - y) * half,
                other_both * rows_w + y * half,
                other_both * rows_w + (1 - y) * half,
                d * rows_w,
                other_x * rows_w,
                other_core * rows_w,
            ]
            + [other_both * rows_w + k * (rows_w // 4) for k in range(4)]
        ).astype(jnp.int32)
        out_rows = (rows_w,) * 3 + (rows_w // 4,) * 4

        def scatter(mine, to_x, to_core, *to_both):
            summed = to_x + jnp.concatenate([over_core(v) for v in to_both], axis=1)
            ahead = [g[0] for g in sent[-1:]]
            return summed, (over_x(after(summed, *ahead)), mine, over_core(to_core))
    else:
        offs = jnp.zeros((2,), jnp.int32)
        out_rows = (size,)

        def gather(w, *ahead):
            return (lax.all_gather(w, "dp", axis=1, tiled=True),)

        def spread(whole):
            return (whole,)

        def scatter(whole):
            return whole, (lax.psum_scatter(whole, "dp", scatter_dimension=1, tiled=True),)

    full_tokens = lax.all_gather(tokens, "tensor")
    ups = [gather(w_up[c * count:(c + 1) * count]) for c in range(chunks)]
    downs = [gather(w_down[c * count:(c + 1) * count], ups[c][-1]) for c in range(chunks)]
    full_cot = lax.all_gather(cotangent, "tensor")

    acts = (hidden, rows, size)
    feats = (tensor, rows, width)
    tiles = [pltpu.VMEM((n, size, size), BF16), pltpu.VMEM((n, size, size), BF16)]
    g_tile = [pltpu.VMEM((n, size, size), F32)]
    product = 6 * rows * size * size

    def cfg(c, lo, first, last):
        return (c * count + lo, n, per, size, len(ups[0]), first, last)

    ups, downs = [spread(*u) for u in ups], [spread(*u) for u in downs]
    if paired:
        ups = [(*u[:-1], over_core(u[-1])) for u in ups]
    state = []
    for c in range(chunks):
        last = c == chunks - 1
        state = call(
            functools.partial(up_kernel, cfg(c, 0, c == 0, last)),
            after(table, downs[c][2]) if paired else table, offs, [full_tokens],
            ups[c], state, [acts, acts] if last else [acts], (), n, size,
            tiles + ([pltpu.VMEM(acts, F32)] if last else []), count * product, 0, count,
        )
    act, slope = state
    if paired:
        downs = [(*u[:-1], over_core(after(u[-1], act))) for u in downs]

    def gate():
        waits = sums[-1:] + [g[0] for g in sent[-2:-1]]
        return after(table, *(waits or downs[-1][1:])) if paired else table

    third = count // 3
    whole = [(c, 0, count) for c in range(chunks)]
    cuts = [(0, 0, third), (0, third, count - third)] + whole[1:] if paired else whole
    state = []
    for c, lo, num in cuts:
        last = c == chunks - 1
        mixed, back, *parts = call(
            functools.partial(down_kernel, cfg(c, lo, not state, last), len(out_rows)),
            gate(), offs, [act, slope, full_cot], downs[c], state, [feats, acts], out_rows, n, size,
            tiles + g_tile, 3 * num * product, lo, num,
        )
        state = [mixed, back]
        summed, grads = scatter(*parts)
        sums.append(summed)
        sent.append(grads)
    mixed_out = lax.psum_scatter(mixed, "tensor", scatter_dimension=0)

    state = []
    for c, lo, num in whole:
        grad, *parts = call(
            functools.partial(end_kernel, cfg(c, lo, not state, False), len(out_rows)),
            gate(), offs, [full_tokens, back], ups[c], state, [feats], out_rows, n, size,
            tiles + g_tile, 2 * num * product, lo, num,
        )
        state = [grad]
        summed, grads = scatter(*parts)
        sums.append(summed)
        sent.append(grads)
    grad_tokens = lax.psum_scatter(grad, "tensor", scatter_dimension=0)

    def join(grads):
        return jnp.concatenate([sum(g[1:], g[0]) for g in grads], axis=0)

    return mixed_out, grad_tokens, join(sent[len(cuts):]), join(sent[:len(cuts)])


def solution(mesh):
    in_specs = (
        P(("group", "dp"), "tensor"),
        P(("group", "dp"), "tensor"),
        P("tensor", "dp", None),
        P("tensor", "dp", None),
        P("tensor", None),
        P("tensor", None),
        P("tensor"),
    )
    out_specs = (
        P(("group", "dp"), "tensor"),
        P(("group", "dp"), "tensor"),
        P(("group", "tensor"), "dp", None),
        P(("group", "tensor"), "dp", None),
    )
    return jax.shard_map(
        functools.partial(on_device, mesh.shape["group"], mesh.shape["dp"]),
        mesh=mesh, in_specs=in_specs, out_specs=out_specs, check_vma=False,
    )
```
